32 devices in a mesh: grp: 2 (over y), row: 4 (over z), col: 2 (over x), rep: 2 (over core).
Axes of the slice: x: 2, y: 2, z: 4, core: 2. Of those that a mesh axis runs over, the one named last changes fastest.
Arguments:
- integrals: bfloat16 [32, 1024, 1024], P(('grp', 'rep'), 'row', 'col'), parts along dimension 0, may hold values from -0.078125 to 0.078125
- density: bfloat16 [2048, 1024], P(('grp', 'row', 'col')), parts along dimension 0, may hold values from -6 to 6
- tile_mask: int32 [4, 16, 16], P(('grp', 'rep'), 'row', 'col'), parts along dimension 0, may hold values 0 or 1
Outputs:
- exchange: bfloat16 [2048, 1024], P(('grp', 'row', 'col', 'rep')), parts along dimension 0
The draws below stay inside these ranges and needn't reach their ends.
There are 2 independent parts, one for each index of `grp`. The reference program is written for one: setup_inputs(seed, part) draws one part's arguments, and reference() takes and returns one part's arrays. A program takes and returns all parts, laid end to end along the dimension named above; each array names one. Nothing has to cross between parts.
All inputs are finite; a program needn't handle non-finite values. No bound on the sum of `tile_mask` on one device may be relied on, other than what follows from the above.
Results may differ from the reference program's by a relative error of at most 0.0049.
Values may be sent and summed in bfloat16 or wider, within the bound.
A program may use at most 64 MiB of HBM per device.

```python
import jax
import jax.numpy as jnp
from jax import lax

N = 1024
TILE = 64
PTILE = 8
AUX_DEV = 1
P_SIZE = 16
NT = 16
PT = 2
N_ROW = 4
N_COL = 2
N_REP = 2


def touch_ends(result, own_key, smallest, largest):
    dims = result.shape
    index_at = [jax.random.randint(jax.random.fold_in(own_key, axis), (), 0, dims[axis]) for axis in range(len(dims))]
    result = result.at[tuple(index_at)].set(smallest)
    longest = dims.index(max(dims))
    index_at[longest] = (index_at[longest] + 1) % dims[longest]
    return result.at[tuple(index_at)].set(largest)


def spiked(entries, rng, source, target, shards_of, factor):
    owner, partner = [(jnp.arange(entries.shape[position]) // (entries.shape[position] // shards_of)).reshape([-1 if axis == position else 1 for axis in range(entries.ndim)]) for position in (source, target)]
    chosen = jax.random.permutation(rng, shards_of)[partner]
    strong = (owner == chosen) | (owner == (partner + shards_of // 2) % shards_of)
    return jnp.where(strong, factor * entries, entries)


def steps_of(key, shape, pieces, smallest, high):
    loudness = 1.0
    for position, shards_of in pieces:
        steps = jax.random.uniform(jax.random.fold_in(jax.random.fold_in(key, 6), position), (shards_of,), jnp.float32, smallest / len(pieces), high / len(pieces))
        loudness = loudness * jnp.repeat(jnp.exp(steps), shape[position] // shards_of).reshape((-1,) + (1,) * (len(shape) - 1 - position))
    return loudness


def gaussian(stream_key, shape, width, bound, split=(), dtype=jnp.bfloat16):
    entries = width * jax.random.normal(stream_key, shape, jnp.float32)
    if split:
        entries = entries * steps_of(stream_key, shape, split, -0.22, 0.18)
    return jnp.clip(entries, -bound, bound).astype(dtype)


def heavy_noise(rng, extent, spread, most, shards, heavy, dtype=jnp.bfloat16):
    entries = spread * jax.random.normal(rng, extent, jnp.float32)
    if shards:
        entries = entries * steps_of(rng, extent, shards, -0.22, 0.18)
    return jnp.clip(spiked(entries, jax.random.fold_in(rng, 3), *heavy), -most, most).astype(dtype)


def setup_inputs(seed: int = 0, part: int = 0) -> dict:
    keys = jax.random.split(jax.random.key(seed), 4)
    part_splits = jax.random.split(jax.random.fold_in(keys[3], part), 4)
    return {
        "integrals": heavy_noise(part_splits[0], (P_SIZE, N, N), (0.0078125 / (AUX_DEV * N_ROW * N_COL * N_REP) ** 0.25), 0.078125, ((0, 2), (1, 4), (2, 2)), (0, 1, 4, 2.0)),
        "density": gaussian(part_splits[1], (N, N), 1.0, 6.0, ((0, 8),)),
        "tile_mask": touch_ends((jax.random.randint(part_splits[2], (PT, NT, NT), 0, 4) < 3).astype(jnp.int32), jax.random.fold_in(part_splits[2], 1), 0, 1),
    }


def reference(integrals, density, tile_mask):
    blocks = integrals.reshape(PT, PTILE, N, N)
    dens32 = density.astype(jnp.float32)

    def step(total, pair):
        block, mask = pair
        big = jnp.repeat(jnp.repeat(mask, TILE, axis=0), TILE, axis=1).astype(jnp.bfloat16)
        screened = block * big[None, :, :]
        s32 = screened.astype(jnp.float32)
        half = jnp.einsum('pmn,ns->pms', s32, dens32).astype(jnp.bfloat16)
        total = total + jnp.einsum('pms,pls->ml', half.astype(jnp.float32), s32)
        return total, None

    total, unused = lax.scan(step, jnp.zeros((N, N), jnp.float32), (blocks, tile_mask))
    return total.astype(jnp.bfloat16)
```

```python
import functools

import jax
import jax.numpy as jnp
from jax import lax
from jax.experimental import pallas as pl
from jax.experimental.pallas import tpu as pltpu
from jax.sharding import PartitionSpec as P

F32 = jnp.float32
BF16 = jnp.bfloat16


def exchange_kernel(
    x_ref, d_ref, mask_ref, out_ref,
    sbuf, owned, dens, half, kf, ks, crecv, xs, xrecv, zs, zrecv, tot,
    a_send, a_recv, dz_send, dz_recv, dx_send, dx_recv, dc_send, dc_recv,
    kc_send, kc_recv, kx_send, kx_recv, kz_send, kz_recv,
):
    r, c, q = lax.axis_index("row"), lax.axis_index("col"), lax.axis_index("rep")
    hi, lo = r // 2, r % 2
    far = [r, hi * 2 + 1 - lo, (1 - hi) * 2 + lo, 3 - r]
    oc, oq = 1 - c, 1 - q
    me = 2 * r + c

    def dev(row, col, rep):
        return {"row": row, "col": col, "rep": rep}

    sends = []

    def copy(src, dst, ssem, rsem, to):
        return pltpu.make_async_remote_copy(
            src_ref=src, dst_ref=dst, send_sem=ssem, recv_sem=rsem,
            device_id=to, device_id_type=pl.DeviceIdType.MESH,
        )

    def send(src, dst, ssem, rsem, to):
        made = copy(src, dst, ssem, rsem, to)
        made.start()
        sends.append(made)

    def arrive(dst, ssem, rsem):
        copy(dst, dst, ssem, rsem, dev(r, c, oq)).wait_recv()

    barrier = pltpu.get_barrier_semaphore()
    partners = [dev(r, c, oq), dev(r, oc, q)]
    for k in (1, 2, 3):
        partners += [dev(far[k], c, q), dev(far[k], oc, q)]
    for to in partners:
        pl.semaphore_signal(barrier, inc=1, device_id=to, device_id_type=pl.DeviceIdType.MESH)

    rows, cols = x_ref.shape[1], x_ref.shape[2]
    tiles_m, tiles_n = mask_ref.shape[1], mask_ref.shape[2]
    tile_m, tile_n = rows // tiles_m, cols // tiles_n
    lane = lax.broadcasted_iota(jnp.int32, (16, cols), 1) // tile_n
    weights = []
    for i in range(tiles_m):
        line = jnp.zeros((16, cols), F32)
        for j in range(tiles_n):
            line = jnp.where(lane == j, mask_ref[0, i, j].astype(F32), line)
        weights.append(line.astype(BF16)[None])

    def screen(f, dst, at):
        for i in range(tiles_m):
            part = x_ref[f, pl.ds(i * tile_m, tile_m), :].reshape(tile_m // 16, 16, cols)
            dst[at, pl.ds(i * tile_m, tile_m), :] = (part * weights[i]).reshape(tile_m, cols)

    hd = d_ref.shape[0] // 2
    for b in range(2):
        dens[2 * me + b] = d_ref[pl.ds(b * hd, hd), :]

    pl.semaphore_wait(barrier, len(partners))

    mine = 2 * me + q
    for k in (3, 2, 1):
        send(dens.at[mine], dens.at[mine], dz_send.at[k], dz_recv.at[k], dev(far[k], c, q))
    send(dens.at[mine], dens.at[mine], dx_send.at[0], dx_recv.at[0], dev(r, oc, q))

    for k in (3, 2, 0, 1):
        for cc in ((oc,) if k == 0 else (c, oc)):
            f = 2 * far[k] + cc
            screen(f, sbuf, f)
            send(sbuf.at[f], owned.at[me], a_send.at[f], a_recv.at[me], dev(far[k], cc, q))
    screen(me, owned, me)

    for k in (1, 2, 3):
        b = 2 * (2 * far[k] + c) + q
        arrive(dens.at[b], dz_send.at[k], dz_recv.at[k])
        send(dens.at[b], dens.at[b], dx_send.at[k], dx_recv.at[k], dev(r, oc, q))
        send(dens.at[b], dens.at[b], dc_send.at[k], dc_recv.at[k], dev(r, c, oq))
    for k in (0, 1, 2, 3):
        b = 2 * (2 * far[k] + oc) + q
        arrive(dens.at[b], dx_send.at[k], dx_recv.at[k])
        send(dens.at[b], dens.at[b], dc_send.at[4 + k], dc_recv.at[4 + k], dev(r, c, oq))
    for k in (1, 2, 3):
        b = 2 * (2 * far[k] + c) + oq
        arrive(dens.at[b], dc_send.at[k], dc_recv.at[k])
    for k in (0, 1, 2, 3):
        b = 2 * (2 * far[k] + oc) + oq
        arrive(dens.at[b], dc_send.at[4 + k], dc_recv.at[4 + k])

    n = d_ref.shape[1]
    hb = dens.shape[0] // 2
    gran = out_ref.shape[0]

    def product(k, j):
        acc = jnp.zeros((rows, rows), F32)
        for cc in range(2):
            acc += lax.dot_general(
                half[k, :, pl.ds(cc * cols, cols)], owned[2 * far[j] + cc],
                (((1,), (1,)), ((), ())), preferred_element_type=F32,
            )
        at = pl.ds(pl.multiple_of(far[j] * rows, rows), rows)
        for c2 in range(2):
            for q2 in range(2):
                part = acc[(2 * c2 + q2) * gran:(2 * c2 + q2 + 1) * gran, :]
                kf[k, q2, c2, :, at] = part
                ks[k, q2, c2, :, at] = part.astype(BF16)

    done = []
    for k in (0, 1, 2, 3):
        for cc in ((oc,) if k == 0 else (c, oc)):
            b = 2 * far[k] + cc
            arrive(owned.at[b], a_send.at[b], a_recv.at[b])
        for s in range(0, n, 256):
            acc = jnp.zeros((rows, 256), F32)
            for cc in range(2):
                block = dens[pl.ds(cc * hb, hb), :, pl.ds(s, 256)].reshape(cols, 256)
                acc += jnp.dot(owned[2 * far[k] + cc], block, preferred_element_type=F32)
            half[k, :, pl.ds(s, 256)] = acc.astype(BF16)
        if k < 3:
            product(k, k)
            for j in done:
                product(k, j)
                product(j, k)
            done.append(k)

    order = (3, 2, 1, 0)

    def stage_a(k):
        for j in ((0, 1, 2, 3) if k == 3 else (3,)):
            product(k, j)
        send(ks.at[k, oq], crecv.at[k], kc_send.at[k], kc_recv.at[k], dev(r, c, oq))

    def stage_b(k):
        arrive(crecv.at[k], kc_send.at[k], kc_recv.at[k])
        xs[k] = (kf[k, q, oc] + crecv[k, oc].astype(F32)).astype(BF16)
        send(xs.at[k], xrecv.at[k], kx_send.at[k], kx_recv.at[k], dev(r, oc, q))

    def stage_c(k):
        arrive(xrecv.at[k], kx_send.at[k], kx_recv.at[k])
        total = kf[k, q, c] + crecv[k, c].astype(F32) + xrecv[k].astype(F32)
        if k:
            zs[k] = total.astype(BF16)
            send(zs.at[k], zrecv.at[k], kz_send.at[k], kz_recv.at[k], dev(far[k], c, q))
        else:
            tot[...] = total

    for t in range(6):
        if t < 4:
            stage_a(order[t])
        if 0 <= t - 1 < 4:
            stage_b(order[t - 1])
        if 0 <= t - 2 < 4:
            stage_c(order[t - 2])
    total = tot[...]
    for k in (1, 2, 3):
        arrive(zrecv.at[k], kz_send.at[k], kz_recv.at[k])
        total += zrecv[k].astype(F32)
    out_ref[...] = total.astype(out_ref.dtype)
    for made in sends:
        made.wait_send()


def fused(integrals, density, tile_mask, gran):
    fns, rows, cols = integrals.shape
    drows, n = density.shape
    dma = pltpu.SemaphoreType.DMA
    vmem = pltpu.VMEM
    flops = 4 * n * n * n
    return pl.pallas_call(
        exchange_kernel,
        out_shape=jax.ShapeDtypeStruct((gran, n), BF16),
        in_specs=[
            pl.BlockSpec(memory_space=pltpu.VMEM),
            pl.BlockSpec(memory_space=pltpu.VMEM),
            pl.BlockSpec(memory_space=pltpu.SMEM),
        ],
        out_specs=pl.BlockSpec(memory_space=pltpu.VMEM),
        scratch_shapes=[
            vmem((fns, rows, cols), BF16),
            vmem((fns, rows, cols), BF16),
            vmem((16, drows // 2, n), BF16),
            vmem((4, rows, n), BF16),
            vmem((4, 2, 2, gran, n), F32),
            vmem((4, 2, 2, gran, n), BF16),
            vmem((4, 2, gran, n), BF16),
            vmem((4, gran, n), BF16),
            vmem((4, gran, n), BF16),
            vmem((4, gran, n), BF16),
            vmem((4, gran, n), BF16),
            vmem((gran, n), F32),
            dma((8,)), dma((8,)), dma((4,)), dma((4,)), dma((4,)), dma((4,)), dma((8,)), dma((8,)),
            dma((4,)), dma((4,)), dma((4,)), dma((4,)), dma((4,)), dma((4,)),
        ],
        compiler_params=pltpu.CompilerParams(
            collective_id=0, has_side_effects=True, vmem_limit_bytes=48 * 1024 * 1024
        ),
        cost_estimate=pl.CostEstimate(flops=flops, bytes_accessed=5 * 1024 * 1024, transcendentals=0),
    )(integrals, density, tile_mask)


def general(integrals, density, tile_mask):
    aux_rows, ao_rows, ao_cols = integrals.shape
    mask_aux, mask_rows, mask_cols = tile_mask.shape
    shaped = integrals.reshape(
        mask_aux,
        aux_rows // mask_aux,
        mask_rows,
        ao_rows // mask_rows,
        mask_cols,
        ao_cols // mask_cols,
    )
    weights = tile_mask.astype(jnp.bfloat16)[:, None, :, None, :, None]
    screened = (shaped * weights).reshape(aux_rows, ao_rows, ao_cols)
    owned = lax.all_to_all(
        lax.all_to_all(screened, "row", split_axis=0, concat_axis=1, tiled=True),
        "col",
        split_axis=0,
        concat_axis=2,
        tiled=True,
    )
    full_density = lax.all_gather(density, ("row", "col"), axis=0, tiled=True)
    half = jnp.einsum(
        "amn,ns->ams", owned, full_density, preferred_element_type=jnp.float32
    ).astype(jnp.bfloat16)
    result = lax.psum_scatter(
        jnp.einsum("ams,als->ml", half, owned, preferred_element_type=jnp.float32),
        ("row", "col", "rep"),
        scatter_dimension=0,
        tiled=True,
    )
    return result.astype(jnp.bfloat16)


def shards(mesh, integrals, density, tile_mask):
    n_row, n_col, n_rep = (mesh.shape[name] for name in ("row", "col", "rep"))
    fns, rows, cols = integrals.shape
    gran = rows // (n_col * n_rep)
    fits = (
        (n_row, n_col, n_rep) == (4, 2, 2)
        and fns == n_row * n_col
        and tile_mask.shape[0] == 1
        and gran % 16 == 0
        and (rows // tile_mask.shape[1]) % 16 == 0
        and rows % 128 == 0
        and cols % 256 == 0
        and density.shape[0] % 32 == 0
    )
    if fits:
        return fused(integrals, density, tile_mask, gran)
    return general(integrals, density, tile_mask)


def solution(mesh):
    placed = (
        P(("grp", "rep"), "row", "col"),
        P(("grp", "row", "col"), None),
        P(("grp", "rep"), "row", "col"),
    )
    return jax.shard_map(
        functools.partial(shards, mesh),
        mesh=mesh,
        in_specs=placed,
        out_specs=P(("grp", "row", "col", "rep"), None),
        check_vma=False,
    )
```

```python
import functools

import jax
import jax.numpy as jnp
from jax import lax
from jax.experimental import pallas as pl
from jax.experimental.pallas import tpu as pltpu
from jax.sharding import PartitionSpec as P

F32 = jnp.float32
BF16 = jnp.bfloat16
A2A_ORDER = ((2, 0), (2, 1), (1, 0), (0, 1), (1, 1), (3, 0), (3, 1))
FIRST, SECOND = 2, 5
ZFIRST = False


EARLY = ((2, 0, 3), (1, 0, 3), (0, 0, 3))
LATE = ((3, 0, 4), (2, 3, 1), (1, 3, 1), (0, 3, 1))


def exchange_kernel(
    x_hbm, d_hbm, mask_ref, out_ref,
    x_ref, owned, dens, half, kf, ks, crecv, xs, xrecv, zs, zrecv, tot,
    x_in, d_in, a_send, a_recv, dz_send, dz_recv, dx_send, dx_recv, dc_send, dc_recv,
    kc_send, kc_recv, kx_send, kx_recv, kz_send, kz_recv,
):
    r, c, q = lax.axis_index("row"), lax.axis_index("col"), lax.axis_index("rep")
    hi, lo = r // 2, r % 2
    far = [r, hi * 2 + 1 - lo, (1 - hi) * 2 + lo, 3 - r]
    oc, oq = 1 - c, 1 - q
    me = 2 * r + c

    def dev(row, col, rep):
        return {"row": row, "col": col, "rep": rep}

    sends = []

    def copy(src, dst, ssem, rsem, to):
        return pltpu.make_async_remote_copy(
            src_ref=src, dst_ref=dst, send_sem=ssem, recv_sem=rsem,
            device_id=to, device_id_type=pl.DeviceIdType.MESH,
        )

    def send(src, dst, ssem, rsem, to):
        made = copy(src, dst, ssem, rsem, to)
        made.start()
        sends.append(made)

    def arrive(dst, ssem, rsem):
        copy(dst, dst, ssem, rsem, dev(r, c, oq)).wait_recv()

    barrier = pltpu.get_barrier_semaphore()
    partners = [dev(r, c, oq), dev(r, oc, q)]
    for k in (1, 2, 3):
        partners += [dev(far[k], c, q), dev(far[k], oc, q)]
    for to in partners:
        pl.semaphore_signal(barrier, inc=1, device_id=to, device_id_type=pl.DeviceIdType.MESH)

    hd = d_hbm.shape[0] // 2
    d_copies = [
        pltpu.make_async_copy(d_hbm.at[pl.ds(b * hd, hd)], dens.at[2 * me + b], d_in.at[b]) for b in range(2)
    ]
    for made in d_copies:
        made.start()
    blocks = {(k, cc): 2 * far[k] + (c, oc)[cc] for k in range(4) for cc in range(2)}
    x_copies = {}
    for at in A2A_ORDER + ((0, 0),):
        f = blocks[at]
        x_copies[at] = pltpu.make_async_copy(x_hbm.at[f], x_ref.at[f], x_in.at[f])
        x_copies[at].start()

    rows, cols = x_ref.shape[1], x_ref.shape[2]
    tiles_m, tiles_n = mask_ref.shape[1], mask_ref.shape[2]
    tile_m, tile_n = rows // tiles_m, cols // tiles_n
    lane = lax.broadcasted_iota(jnp.int32, (16, cols), 1) // tile_n
    weights = []
    for i in range(tiles_m):
        line = jnp.zeros((16, cols), F32)
        for j in range(tiles_n):
            line = jnp.where(lane == j, mask_ref[0, i, j].astype(F32), line)
        weights.append(line.astype(BF16)[None])

    def screen(at, dst, place):
        f = blocks[at]
        x_copies[at].wait()
        for i in range(tiles_m):
            part = x_ref[f, pl.ds(i * tile_m, tile_m), :].reshape(tile_m // 16, 16, cols)
            dst[place, pl.ds(i * tile_m, tile_m), :] = (part * weights[i]).reshape(tile_m, cols)

    ready = set()

    def to_owner(at):
        f = blocks[at]
        if at not in ready:
            screen(at, x_ref, f)
            ready.add(at)
        send(x_ref.at[f], owned.at[me], a_send.at[f], a_recv.at[me], dev(far[at[0]], (c, oc)[at[1]], q))

    for made in d_copies:
        made.wait()
    screen(A2A_ORDER[0], x_ref, blocks[A2A_ORDER[0]])
    ready.add(A2A_ORDER[0])
    pl.semaphore_wait(barrier, len(partners))

    mine = 2 * me + q
    for k in (2, 1):
        send(dens.at[mine], dens.at[mine], dz_send.at[k], dz_recv.at[k], dev(far[k], c, q))
    send(dens.at[mine], dens.at[mine], dx_send.at[0], dx_recv.at[0], dev(r, oc, q))
    for at in A2A_ORDER[:FIRST]:
        to_owner(at)
    screen((0, 0), owned, me)

    def dens_z(k):
        b = 2 * (2 * far[k] + c) + q
        arrive(dens.at[b], dz_send.at[k], dz_recv.at[k])
        if k == 2:
            send(dens.at[b], dens.at[b], dz_send.at[3], dz_recv.at[3], dev(far[1], c, q))
        send(dens.at[b], dens.at[b], dx_send.at[k], dx_recv.at[k], dev(r, oc, q))
        send(dens.at[b], dens.at[b], dc_send.at[k], dc_recv.at[k], dev(r, c, oq))

    def dens_x(k):
        b = 2 * (2 * far[k] + oc) + q
        arrive(dens.at[b], dx_send.at[k], dx_recv.at[k])
        send(dens.at[b], dens.at[b], dc_send.at[4 + k], dc_recv.at[4 + k], dev(r, c, oq))

    dens_z(1)
    dens_z(2)
    for at in A2A_ORDER[FIRST:SECOND]:
        to_owner(at)
    dens_z(3)
    for at in A2A_ORDER[SECOND:]:
        to_owner(at)
    for k in (0, 1, 2, 3):
        dens_x(k)
    for k in (1, 2, 3):
        b = 2 * (2 * far[k] + c) + oq
        arrive(dens.at[b], dc_send.at[k], dc_recv.at[k])
    for k in (0, 1, 2, 3):
        b = 2 * (2 * far[k] + oc) + oq
        arrive(dens.at[b], dc_send.at[4 + k], dc_recv.at[4 + k])

    n = d_hbm.shape[1]
    hb = dens.shape[0] // 2
    gran = out_ref.shape[0]

    def product(k, j):
        acc = jnp.zeros((rows, rows), F32)
        for cc in range(2):
            acc += lax.dot_general(
                half[k, :, pl.ds(cc * cols, cols)], owned[2 * far[j] + cc],
                (((1,), (1,)), ((), ())), preferred_element_type=F32,
            )
        for c2 in range(2):
            for q2 in range(2):
                part = acc[(2 * c2 + q2) * gran:(2 * c2 + q2 + 1) * gran, :]
                kf[k, q2, j, c2] = part
                ks[k, q2, j, c2] = part.astype(BF16)

    def row_block(k):
        for cc in ((1,) if k == 0 else (0, 1)):
            b = blocks[(k, cc)]
            arrive(owned.at[b], a_send.at[b], a_recv.at[b])
        for s in range(0, n, 256):
            acc = jnp.zeros((rows, 256), F32)
            for cc in range(2):
                block = dens[pl.ds(cc * hb, hb), :, pl.ds(s, 256)].reshape(cols, 256)
                acc += jnp.dot(owned[2 * far[k] + cc], block, preferred_element_type=F32)
            half[k, :, pl.ds(s, 256)] = acc.astype(BF16)

    def place(item):
        k, j, size = item
        return (EARLY + LATE).index(item), k, pl.ds(j, size)

    def over_core(item):
        i, k, js = place(item)
        send(ks.at[k, oq, js], crecv.at[k, js], kc_send.at[i], kc_recv.at[i], dev(r, c, oq))

    def over_x(item):
        i, k, js = place(item)
        arrive(crecv.at[k, js], kc_send.at[i], kc_recv.at[i])
        xs[k, js] = (kf[k, q, js, oc] + crecv[k, js, oc].astype(F32)).astype(BF16)
        send(xs.at[k, js], xrecv.at[k, js], kx_send.at[i], kx_recv.at[i], dev(r, oc, q))

    def over_z(item):
        i, k, js = place(item)
        arrive(xrecv.at[k, js], kx_send.at[i], kx_recv.at[i])
        total = kf[k, q, js, c] + crecv[k, js, c].astype(F32) + xrecv[k, js].astype(F32)
        if k:
            zs[k, js] = total.astype(BF16)
            send(zs.at[k, js], zrecv.at[k, js], kz_send.at[i], kz_recv.at[i], dev(far[k], c, q))
        else:
            tot[js] = total

    for k in range(3):
        row_block(k)
        for j in range(k):
            product(k, j)
            product(j, k)
        product(k, k)
    for item in EARLY:
        over_core(item)
    for item in EARLY:
        over_x(item)
    if ZFIRST:
        for item in EARLY:
            over_z(item)
    row_block(3)
    for j in range(4):
        product(3, j)
    over_core(LATE[0])
    for k in (2, 1, 0):
        product(k, 3)
        over_core(LATE[3 - k])
    if not ZFIRST:
        for item in EARLY:
            over_z(item)
    for item in LATE:
        over_x(item)
    for item in LATE:
        over_z(item)
    for item in EARLY + LATE:
        i, k, js = place(item)
        if k:
            arrive(zrecv.at[k, js], kz_send.at[i], kz_recv.at[i])
    for j in range(4):
        total = tot[j]
        for k in (1, 2, 3):
            total += zrecv[k, k ^ j].astype(F32)
        at = pl.ds(pl.multiple_of(far[j] * rows, rows), rows)
        out_ref[:, at] = total.astype(out_ref.dtype)
    for made in sends:
        made.wait_send()


def fused(integrals, density, tile_mask, gran):
    fns, rows, cols = integrals.shape
    drows, n = density.shape
    dma = pltpu.SemaphoreType.DMA
    vmem = pltpu.VMEM
    return pl.pallas_call(
        exchange_kernel,
        out_shape=jax.ShapeDtypeStruct((gran, n), BF16),
        in_specs=[
            pl.BlockSpec(memory_space=pl.ANY),
            pl.BlockSpec(memory_space=pl.ANY),
            pl.BlockSpec(memory_space=pltpu.SMEM),
        ],
        out_specs=pl.BlockSpec(memory_space=pltpu.VMEM),
        scratch_shapes=[
            vmem((fns, rows, cols), BF16),
            vmem((fns, rows, cols), BF16),
            vmem((16, drows // 2, n), BF16),
            vmem((4, rows, n), BF16),
            vmem((4, 2, 4, 2, gran, rows), F32),
            vmem((4, 2, 4, 2, gran, rows), BF16),
            vmem((4, 4, 2, gran, rows), BF16),
            vmem((4, 4, gran, rows), BF16),
            vmem((4, 4, gran, rows), BF16),
            vmem((4, 4, gran, rows), BF16),
            vmem((4, 4, gran, rows), BF16),
            vmem((4, gran, rows), F32),
            dma((8,)), dma((2,)), dma((8,)), dma((8,)), dma((4,)), dma((4,)), dma((4,)), dma((4,)), dma((8,)), dma((8,)),
            dma((7,)), dma((7,)), dma((7,)), dma((7,)), dma((7,)), dma((7,)),
        ],
        compiler_params=pltpu.CompilerParams(
            collective_id=0, has_side_effects=True, vmem_limit_bytes=60 * 1024 * 1024
        ),
        cost_estimate=pl.CostEstimate(flops=4 * n * n * n, bytes_accessed=5 * 1024 * 1024, transcendentals=0),
    )(integrals, density, tile_mask)


def general(integrals, density, tile_mask):
    aux_rows, ao_rows, ao_cols = integrals.shape
    mask_aux, mask_rows, mask_cols = tile_mask.shape
    shaped = integrals.reshape(
        mask_aux,
        aux_rows // mask_aux,
        mask_rows,
        ao_rows // mask_rows,
        mask_cols,
        ao_cols // mask_cols,
    )
    weights = tile_mask.astype(jnp.bfloat16)[:, None, :, None, :, None]
    screened = (shaped * weights).reshape(aux_rows, ao_rows, ao_cols)
    owned = lax.all_to_all(
        lax.all_to_all(screened, "row", split_axis=0, concat_axis=1, tiled=True),
        "col",
        split_axis=0,
        concat_axis=2,
        tiled=True,
    )
    full_density = lax.all_gather(density, ("row", "col"), axis=0, tiled=True)
    half = jnp.einsum(
        "amn,ns->ams", owned, full_density, preferred_element_type=jnp.float32
    ).astype(jnp.bfloat16)
    result = lax.psum_scatter(
        jnp.einsum("ams,als->ml", half, owned, preferred_element_type=jnp.float32),
        ("row", "col", "rep"),
        scatter_dimension=0,
        tiled=True,
    )
    return result.astype(jnp.bfloat16)


def shards(mesh, integrals, density, tile_mask):
    n_row, n_col, n_rep = (mesh.shape[name] for name in ("row", "col", "rep"))
    fns, rows, cols = integrals.shape
    gran = rows // (n_col * n_rep)
    fits = (
        (n_row, n_col, n_rep) == (4, 2, 2)
        and fns == n_row * n_col
        and tile_mask.shape[0] == 1
        and gran % 16 == 0
        and (rows // tile_mask.shape[1]) % 16 == 0
        and rows % 128 == 0
        and cols % 256 == 0
        and density.shape[0] % 32 == 0
    )
    if fits:
        return fused(integrals, density, tile_mask, gran)
    return general(integrals, density, tile_mask)


def solution(mesh):
    placed = (
        P(("grp", "rep"), "row", "col"),
        P(("grp", "row", "col"), None),
        P(("grp", "rep"), "row", "col"),
    )
    return jax.shard_map(
        functools.partial(shards, mesh),
        mesh=mesh,
        in_specs=placed,
        out_specs=P(("grp", "row", "col", "rep"), None),
        check_vma=False,
    )
```

```python
import functools

import jax
import jax.numpy as jnp
from jax import lax
from jax.experimental import pallas as pl
from jax.experimental.pallas import tpu as pltpu
from jax.sharding import PartitionSpec as P

F32 = jnp.float32
BF16 = jnp.bfloat16
A2A_ORDER = ((2, 0), (2, 1), (1, 0), (0, 1), (1, 1), (3, 0), (3, 1))
FIRST, SECOND = 2, 5


EARLY = ((2, 0, 3), (1, 0, 3), (0, 0, 3))
LATE = ((3, 0, 2), (3, 2, 2), (2, 3, 1), (1, 3, 1), (0, 3, 1))


def exchange_kernel(
    x_hbm, d_hbm, mask_ref, out_ref,
    x_ref, owned, dens, half, kf, ks, crecv, xs, xrecv, zs, zrecv, tot,
    x_in, d_in, a_send, a_recv, dz_send, dz_recv, dx_send, dx_recv, dc_send, dc_recv,
    kc_send, kc_recv, kx_send, kx_recv, kz_send, kz_recv,
):
    r, c, q = lax.axis_index("row"), lax.axis_index("col"), lax.axis_index("rep")
    hi, lo = r // 2, r % 2
    far = [r, hi * 2 + 1 - lo, (1 - hi) * 2 + lo, 3 - r]
    oc, oq = 1 - c, 1 - q
    me = 2 * r + c

    def dev(row, col, rep):
        return {"row": row, "col": col, "rep": rep}

    sends = []

    def copy(src, dst, ssem, rsem, to):
        return pltpu.make_async_remote_copy(
            src_ref=src, dst_ref=dst, send_sem=ssem, recv_sem=rsem,
            device_id=to, device_id_type=pl.DeviceIdType.MESH,
        )

    def send(src, dst, ssem, rsem, to):
        made = copy(src, dst, ssem, rsem, to)
        made.start()
        sends.append(made)

    def arrive(dst, ssem, rsem):
        copy(dst, dst, ssem, rsem, dev(r, c, oq)).wait_recv()

    barrier = pltpu.get_barrier_semaphore()
    partners = [dev(r, c, oq), dev(r, oc, q)]
    for k in (1, 2, 3):
        partners += [dev(far[k], c, q), dev(far[k], oc, q)]
    for to in partners:
        pl.semaphore_signal(barrier, inc=1, device_id=to, device_id_type=pl.DeviceIdType.MESH)

    hd = d_hbm.shape[0] // 2
    d_copies = [
        pltpu.make_async_copy(d_hbm.at[pl.ds(b * hd, hd)], dens.at[2 * me + b], d_in.at[b]) for b in range(2)
    ]
    for made in d_copies:
        made.start()
    blocks = {(k, cc): 2 * far[k] + (c, oc)[cc] for k in range(4) for cc in range(2)}
    x_copies = {}
    for at in A2A_ORDER + ((0, 0),):
        f = blocks[at]
        x_copies[at] = pltpu.make_async_copy(x_hbm.at[f], x_ref.at[f], x_in.at[f])
        x_copies[at].start()

    rows, cols = x_ref.shape[1], x_ref.shape[2]
    tiles_m, tiles_n = mask_ref.shape[1], mask_ref.shape[2]
    tile_m, tile_n = rows // tiles_m, cols // tiles_n
    lane = lax.broadcasted_iota(jnp.int32, (16, cols), 1) // tile_n
    weights = []
    for i in range(tiles_m):
        line = jnp.zeros((16, cols), F32)
        for j in range(tiles_n):
            line = jnp.where(lane == j, mask_ref[0, i, j].astype(F32), line)
        weights.append(line.astype(BF16)[None])

    def screen(at, dst, place):
        f = blocks[at]
        x_copies[at].wait()
        for i in range(tiles_m):
            part = x_ref[f, pl.ds(i * tile_m, tile_m), :].reshape(tile_m // 16, 16, cols)
            dst[place, pl.ds(i * tile_m, tile_m), :] = (part * weights[i]).reshape(tile_m, cols)

    ready = set()

    def to_owner(at):
        f = blocks[at]
        if at not in ready:
            screen(at, x_ref, f)
            ready.add(at)
        send(x_ref.at[f], owned.at[me], a_send.at[f], a_recv.at[me], dev(far[at[0]], (c, oc)[at[1]], q))

    for made in d_copies:
        made.wait()
    screen(A2A_ORDER[0], x_ref, blocks[A2A_ORDER[0]])
    ready.add(A2A_ORDER[0])
    pl.semaphore_wait(barrier, len(partners))

    mine = 2 * me + q
    for k in (2, 1):
        send(dens.at[mine], dens.at[mine], dz_send.at[k], dz_recv.at[k], dev(far[k], c, q))
    send(dens.at[mine], dens.at[mine], dx_send.at[0], dx_recv.at[0], dev(r, oc, q))
    for at in A2A_ORDER[:FIRST]:
        to_owner(at)
    screen((0, 0), owned, me)

    def dens_z(k):
        b = 2 * (2 * far[k] + c) + q
        arrive(dens.at[b], dz_send.at[k], dz_recv.at[k])
        if k == 2:
            send(dens.at[b], dens.at[b], dz_send.at[3], dz_recv.at[3], dev(far[1], c, q))
        send(dens.at[b], dens.at[b], dx_send.at[k], dx_recv.at[k], dev(r, oc, q))
        send(dens.at[b], dens.at[b], dc_send.at[k], dc_recv.at[k], dev(r, c, oq))

    def dens_x(k):
        b = 2 * (2 * far[k] + oc) + q
        arrive(dens.at[b], dx_send.at[k], dx_recv.at[k])
        send(dens.at[b], dens.at[b], dc_send.at[4 + k], dc_recv.at[4 + k], dev(r, c, oq))

    dens_z(1)
    dens_z(2)
    for at in A2A_ORDER[FIRST:SECOND]:
        to_owner(at)
    dens_z(3)
    for at in A2A_ORDER[SECOND:]:
        to_owner(at)
    for k in (0, 1, 2, 3):
        dens_x(k)
    for k in (1, 2, 3):
        b = 2 * (2 * far[k] + c) + oq
        arrive(dens.at[b], dc_send.at[k], dc_recv.at[k])
    for k in (0, 1, 2, 3):
        b = 2 * (2 * far[k] + oc) + oq
        arrive(dens.at[b], dc_send.at[4 + k], dc_recv.at[4 + k])

    n = d_hbm.shape[1]
    hb = dens.shape[0] // 2
    gran = out_ref.shape[0]

    def product(k, j):
        acc = jnp.zeros((rows, rows), F32)
        for cc in range(2):
            acc += lax.dot_general(
                half[k, :, pl.ds(cc * cols, cols)], owned[2 * far[j] + cc],
                (((1,), (1,)), ((), ())), preferred_element_type=F32,
            )
        for c2 in range(2):
            for q2 in range(2):
                part = acc[(2 * c2 + q2) * gran:(2 * c2 + q2 + 1) * gran, :]
                kf[k, q2, j, c2] = part
                ks[k, q2, j, c2] = part.astype(BF16)

    def landed(k):
        for cc in ((1,) if k == 0 else (0, 1)):
            b = blocks[(k, cc)]
            arrive(owned.at[b], a_send.at[b], a_recv.at[b])

    def half_block(k):
        for s in range(0, n, 256):
            acc = jnp.zeros((rows, 256), F32)
            for cc in range(2):
                block = dens[pl.ds(cc * hb, hb), :, pl.ds(s, 256)].reshape(cols, 256)
                acc += jnp.dot(owned[2 * far[k] + cc], block, preferred_element_type=F32)
            half[k, :, pl.ds(s, 256)] = acc.astype(BF16)

    def place(item):
        k, j, size = item
        return (EARLY + LATE).index(item), k, pl.ds(j, size)

    def over_core(item):
        i, k, js = place(item)
        send(ks.at[k, oq, js], crecv.at[k, js], kc_send.at[i], kc_recv.at[i], dev(r, c, oq))

    def over_x(item):
        i, k, js = place(item)
        arrive(crecv.at[k, js], kc_send.at[i], kc_recv.at[i])
        xs[k, js] = (kf[k, q, js, oc] + crecv[k, js, oc].astype(F32)).astype(BF16)
        send(xs.at[k, js], xrecv.at[k, js], kx_send.at[i], kx_recv.at[i], dev(r, oc, q))

    def over_z(item):
        i, k, js = place(item)
        arrive(xrecv.at[k, js], kx_send.at[i], kx_recv.at[i])
        total = kf[k, q, js, c] + crecv[k, js, c].astype(F32) + xrecv[k, js].astype(F32)
        if k:
            zs[k, js] = total.astype(BF16)
            send(zs.at[k, js], zrecv.at[k, js], kz_send.at[i], kz_recv.at[i], dev(far[k], c, q))
        else:
            tot[js] = total

    for k in range(3):
        landed(k)
        half_block(k)
        for j in range(k):
            product(k, j)
            product(j, k)
        product(k, k)
    for item in EARLY:
        over_core(item)
    for item in EARLY:
        over_x(item)
    landed(3)
    over_z(EARLY[0])
    half_block(3)
    for item in LATE:
        k, j, size = item
        for at in range(j, j + size):
            product(k, at)
        over_core(item)
    for item in EARLY[1:]:
        over_z(item)
    for item in LATE:
        over_x(item)
    for item in LATE:
        over_z(item)
    for item in EARLY + LATE:
        i, k, js = place(item)
        if k:
            arrive(zrecv.at[k, js], kz_send.at[i], kz_recv.at[i])
    for j in range(4):
        total = tot[j]
        for k in (1, 2, 3):
            total += zrecv[k, k ^ j].astype(F32)
        at = pl.ds(pl.multiple_of(far[j] * rows, rows), rows)
        out_ref[:, at] = total.astype(out_ref.dtype)
    for made in sends:
        made.wait_send()


def fused(integrals, density, tile_mask, gran):
    fns, rows, cols = integrals.shape
    drows, n = density.shape
    dma = pltpu.SemaphoreType.DMA
    vmem = pltpu.VMEM
    return pl.pallas_call(
        exchange_kernel,
        out_shape=jax.ShapeDtypeStruct((gran, n), BF16),
        in_specs=[
            pl.BlockSpec(memory_space=pl.ANY),
            pl.BlockSpec(memory_space=pl.ANY),
            pl.BlockSpec(memory_space=pltpu.SMEM),
        ],
        out_specs=pl.BlockSpec(memory_space=pltpu.VMEM),
        scratch_shapes=[
            vmem((fns, rows, cols), BF16),
            vmem((fns, rows, cols), BF16),
            vmem((16, drows // 2, n), BF16),
            vmem((4, rows, n), BF16),
            vmem((4, 2, 4, 2, gran, rows), F32),
            vmem((4, 2, 4, 2, gran, rows), BF16),
            vmem((4, 4, 2, gran, rows), BF16),
            vmem((4, 4, gran, rows), BF16),
            vmem((4, 4, gran, rows), BF16),
            vmem((4, 4, gran, rows), BF16),
            vmem((4, 4, gran, rows), BF16),
            vmem((4, gran, rows), F32),
            dma((8,)), dma((2,)), dma((8,)), dma((8,)), dma((4,)), dma((4,)), dma((4,)), dma((4,)), dma((8,)), dma((8,)),
            dma((len(EARLY + LATE),)), dma((len(EARLY + LATE),)), dma((len(EARLY + LATE),)), dma((len(EARLY + LATE),)), dma((len(EARLY + LATE),)), dma((len(EARLY + LATE),)),
        ],
        compiler_params=pltpu.CompilerParams(
            collective_id=0, has_side_effects=True, vmem_limit_bytes=60 * 1024 * 1024
        ),
        cost_estimate=pl.CostEstimate(flops=4 * n * n * n, bytes_accessed=5 * 1024 * 1024, transcendentals=0),
    )(integrals, density, tile_mask)


def general(integrals, density, tile_mask):
    aux_rows, ao_rows, ao_cols = integrals.shape
    mask_aux, mask_rows, mask_cols = tile_mask.shape
    shaped = integrals.reshape(
        mask_aux,
        aux_rows // mask_aux,
        mask_rows,
        ao_rows // mask_rows,
        mask_cols,
        ao_cols // mask_cols,
    )
    weights = tile_mask.astype(jnp.bfloat16)[:, None, :, None, :, None]
    screened = (shaped * weights).reshape(aux_rows, ao_rows, ao_cols)
    owned = lax.all_to_all(
        lax.all_to_all(screened, "row", split_axis=0, concat_axis=1, tiled=True),
        "col",
        split_axis=0,
        concat_axis=2,
        tiled=True,
    )
    full_density = lax.all_gather(density, ("row", "col"), axis=0, tiled=True)
    half = jnp.einsum(
        "amn,ns->ams", owned, full_density, preferred_element_type=jnp.float32
    ).astype(jnp.bfloat16)
    result = lax.psum_scatter(
        jnp.einsum("ams,als->ml", half, owned, preferred_element_type=jnp.float32),
        ("row", "col", "rep"),
        scatter_dimension=0,
        tiled=True,
    )
    return result.astype(jnp.bfloat16)


def shards(mesh, integrals, density, tile_mask):
    n_row, n_col, n_rep = (mesh.shape[name] for name in ("row", "col", "rep"))
    fns, rows, cols = integrals.shape
    gran = rows // (n_col * n_rep)
    fits = (
        (n_row, n_col, n_rep) == (4, 2, 2)
        and fns == n_row * n_col
        and tile_mask.shape[0] == 1
        and gran % 16 == 0
        and (rows // tile_mask.shape[1]) % 16 == 0
        and rows % 128 == 0
        and cols % 256 == 0
        and density.shape[0] % 32 == 0
    )
    if fits:
        return fused(integrals, density, tile_mask, gran)
    return general(integrals, density, tile_mask)


def solution(mesh):
    placed = (
        P(("grp", "rep"), "row", "col"),
        P(("grp", "row", "col"), None),
        P(("grp", "rep"), "row", "col"),
    )
    return jax.shard_map(
        functools.partial(shards, mesh),
        mesh=mesh,
        in_specs=placed,
        out_specs=P(("grp", "row", "col", "rep"), None),
        check_vma=False,
    )
```
